256 devices in a mesh: dp: 64 (over x, z, core), expert: 4 (over y).
Axes of the slice: x: 4, y: 4, z: 8, core: 2. Of those that a mesh axis runs over, the one named last changes fastest.
Arguments:
- grad: bfloat16 [16, 7168, 2048], P('expert', 'dp')
- momentum: float32 [16, 7168, 2048], P('expert', 'dp'), may hold values from -6 to 6
- placement: int32 [16], replicated, may hold values from 0 to 15, as said below
Outputs:
- momentum_new: float32 [16, 7168, 2048], P('expert', 'dp')
- update: bfloat16 [16, 7168, 2048], P('expert', 'dp')
The draws below stay inside these ranges and needn't reach their ends.
Inputs may be any that keep to these rules, and one draw needn't show every extreme that they name: placement is a permutation; position e lies in group e // 4, and placement[e] // 4 is the new group. The 4 experts of each group go to 4 different groups, so every group receives exactly one expert from every group.
All inputs are finite; a program needn't handle non-finite values.
Results may differ from the reference program's by a relative error of at most 0.0074.
Values may be sent and summed in bfloat16 or wider, within the bound.
A program may use at most 128 MiB of HBM per device.

```python
import math
import jax
import jax.numpy as jnp
from jax import lax

D = 7168
FF = 2048
LOCAL = 4
EXPERTS = 16


def draw_grad(key, part):
    key = jax.random.fold_in(key, 11)
    key_base, key_rows, key_cols = jax.random.split(key, 3)
    base = jnp.clip(jax.random.normal(key_base, (EXPERTS, D, FF), jnp.float32), -6.0, 6.0)
    row_scale = jnp.exp(jax.random.uniform(key_rows, (EXPERTS, D, 1), jnp.float32, 0.0, math.log(10.0)))
    col_scale = jnp.exp(jax.random.uniform(key_cols, (EXPERTS, 1, FF), jnp.float32, 0.0, math.log(3.0)))
    return (base * row_scale * col_scale).astype(jnp.bfloat16)


def draw_placement(key, part):
    key = jax.random.fold_in(key, 23)
    key_slot, key_source, key_block = jax.random.split(key, 3)
    perm_slot = jax.random.permutation(key_slot, LOCAL)
    perm_source = jax.random.permutation(key_source, LOCAL)
    perm_block = jax.random.permutation(key_block, LOCAL)
    sources = jnp.arange(LOCAL, dtype=jnp.int32)[:, None]
    slot_ids = jnp.arange(LOCAL, dtype=jnp.int32)[None, :]
    targets = (perm_slot[slot_ids] + perm_source[sources]) % LOCAL
    new_slot = (perm_block[sources] + targets) % LOCAL
    return (targets * LOCAL + new_slot).reshape(-1).astype(jnp.int32)


def level_of(key, extent, cuts, smallest, top_value):
    gain = 1.0
    for dim, shards_of in cuts:
        heights = jax.random.uniform(jax.random.fold_in(jax.random.fold_in(key, 6), dim), (shards_of,), jnp.float32, smallest / len(cuts), top_value / len(cuts))
        gain = gain * jnp.repeat(jnp.exp(heights), extent[dim] // shards_of).reshape((-1,) + (1,) * (len(extent) - 1 - dim))
    return gain


def normal_values(own_key, extent, spread, reach, pieces=(), kind=jnp.bfloat16):
    loudness = level_of(own_key, extent, pieces, -0.22, 0.18) if pieces else 1.0
    entries = jax.random.normal(own_key, extent, jnp.float32) * spread * loudness
    return jnp.minimum(jnp.maximum(entries, -reach), reach).astype(kind)


def setup_inputs(seed: int = 0) -> dict:
    keys = jax.random.split(jax.random.key(seed), 4)
    grad = draw_grad(jax.random.fold_in(keys[3], 71), 0)
    momentum = normal_values(keys[1], (EXPERTS, D, FF), 1.0, 6.0, ((0, 4), (1, 64)), jnp.float32)
    placement = draw_placement(jax.random.fold_in(keys[3], 71), 0)
    return dict(grad=grad, momentum=momentum, placement=placement)


def orthogonalize(moved_one):
    values = moved_one.astype(jnp.float32)
    squares = jnp.sum(values * values)
    factor = 0.5 * math.sqrt(FF) / jnp.sqrt(squares + 1e-06)
    normal = (values * factor).astype(jnp.bfloat16)
    gram_whole = jnp.dot(normal.T, normal, preferred_element_type=jnp.float32).astype(jnp.bfloat16)
    product = jnp.dot(normal, gram_whole, preferred_element_type=jnp.float32).astype(jnp.bfloat16)
    second = jnp.dot(product, gram_whole, preferred_element_type=jnp.float32)
    orthogonal = 3.4445 * normal.astype(jnp.float32) - 4.775 * product.astype(jnp.float32) + 2.0315 * second
    return (orthogonal * math.sqrt(D)).astype(jnp.bfloat16)

def reference(grad, momentum, placement):
    momentum_new = 0.95 * momentum + grad.astype(jnp.float32)
    moved = momentum_new.astype(jnp.bfloat16)
    results = lax.map(orthogonalize, moved)
    update = jnp.zeros_like(results).at[placement.astype(jnp.int32)].set(results)
    return (momentum_new, update)
```

```python
import functools
import math

import jax
import jax.numpy as jnp
from jax import lax
from jax.experimental import pallas as pl
from jax.experimental.pallas import tpu as pltpu
from jax.sharding import PartitionSpec as P

D = 7168
MESH = pl.DeviceIdType.MESH
LOCAL = 4
RING = 8
ROWS = 112
OWNED = LOCAL * ROWS
FF = 2048
CHUNK = FF // RING
HALF = CHUNK // 2
WIDE = LOCAL * CHUNK
STRIP = WIDE + HALF
PART = HALF // 2


def prep_kernel(slots_ref, grad_ref, momentum_ref, new_ref, out_ref):
    new = 0.95 * momentum_ref[0] + grad_ref[0].astype(jnp.float32)
    new_ref[0] = new
    moved = new.astype(jnp.bfloat16)
    for q in range(out_ref.shape[0]):
        out_ref[q, 0] = moved[:, q * CHUNK : (q + 1) * CHUNK]


def prepare(slots, grad, momentum):
    halves = 2
    columns = FF // halves
    taken = pl.BlockSpec((1, ROWS, columns), lambda i, h, slots: (slots[i], 0, h))
    return pl.pallas_call(
        prep_kernel,
        grid_spec=pltpu.PrefetchScalarGridSpec(
            num_scalar_prefetch=1,
            grid=(LOCAL, halves),
            in_specs=[taken, taken],
            out_specs=[
                taken,
                pl.BlockSpec((RING // halves, 1, ROWS, CHUNK), lambda i, h, slots: (h, i, 0, 0)),
            ],
        ),
        out_shape=[
            jax.ShapeDtypeStruct((LOCAL, ROWS, FF), jnp.float32),
            jax.ShapeDtypeStruct((RING, LOCAL, ROWS, CHUNK), jnp.bfloat16),
        ],
        compiler_params=pltpu.CompilerParams(vmem_limit_bytes=32 << 20),
        name="prepare",
    )(slots, grad, momentum)


def place_kernel(sources_ref, from_ref, to_ref):
    to_ref[...] = from_ref[...]


def place(sources, returned):
    return pl.pallas_call(
        place_kernel,
        grid_spec=pltpu.PrefetchScalarGridSpec(
            num_scalar_prefetch=1,
            grid=(LOCAL,),
            in_specs=[pl.BlockSpec((1, ROWS, FF), lambda i, sources: (sources[i], 0, 0))],
            out_specs=pl.BlockSpec((1, ROWS, FF), lambda i, sources: (i, 0, 0)),
        ),
        out_shape=jax.ShapeDtypeStruct((LOCAL, ROWS, FF), jnp.bfloat16),
        name="place",
    )(sources, returned)


def muon_kernel(
    outgoing,
    result,
    by_source,
    rows,
    squares,
    part,
    send_sum,
    recv_sum,
    strips,
    gram,
    normal,
    product,
    done,
    y_send,
    y_recv,
    x_send,
    x_recv,
    twin_send,
    twin_recv,
    sq_send,
    sq_recv,
    sum_send,
    sum_recv,
    all_send,
    all_recv,
    all_twin_send,
    all_twin_recv,
    back_send,
    back_recv,
):
    dp = lax.axis_index("dp")
    y = lax.axis_index("expert")
    x, z, core = dp // 16, (dp // 2) % RING, dp % 2

    def device(to_x, to_y, to_z, to_core):
        return (to_x * 16 + to_z * 2 + to_core, to_y)

    def turn(value, by, size):
        return lax.rem(value + (by % size), size)

    def remote(source, target, send, recv, where):
        return pltpu.make_async_remote_copy(
            src_ref=source,
            dst_ref=target,
            send_sem=send,
            recv_sem=recv,
            device_id=where,
            device_id_type=MESH,
        )

    def arrived(ref, sem):
        pltpu.make_async_copy(ref, ref, sem).wait()

    along_x = [turn(x, e, LOCAL) for e in range(LOCAL)]
    along_y = [turn(y, e, LOCAL) for e in range(LOCAL)]
    twin = device(x, y, z, 1 - core)

    barrier = pltpu.get_barrier_semaphore()
    partners = (
        [device(to, y, z, core) for to in along_x[1:]]
        + [device(x, to, z, core) for to in along_y[1:]]
        + [device(x, y, turn(z, e, RING), core) for e in range(1, RING)]
        + [twin]
    )
    for partner in partners:
        pl.semaphore_signal(barrier, inc=1, device_id=partner, device_id_type=MESH)
    pl.semaphore_wait(barrier, len(partners))

    pending = []

    chunks = [turn(z, 4 + t, RING) for t in range(RING)]
    for t, q in enumerate(chunks):
        for to in along_y[1:]:
            copy = remote(
                outgoing.at[q, to],
                by_source.at[q, y],
                y_send.at[t, to],
                y_recv.at[t, y],
                device(x, to, z, core),
            )
            copy.start()
            pending.append(copy)
        pltpu.make_async_copy(outgoing.at[q, y], by_source.at[q, y], y_recv.at[t, y]).start()

    def pass_on(t):
        q = chunks[t]
        for to in along_x[1:]:
            arrived(by_source.at[q, to], y_recv.at[t, to])
            copy = remote(
                by_source.at[q, to],
                rows.at[q, core, pl.ds(pl.multiple_of(x * ROWS, 16), ROWS)],
                x_send.at[t, to],
                x_recv.at[t, x],
                device(to, y, z, core),
            )
            copy.start()
            pending.append(copy)
        arrived(by_source.at[q, x], y_recv.at[t, x])
        pltpu.make_async_copy(
            by_source.at[q, x],
            rows.at[q, core, pl.ds(pl.multiple_of(x * ROWS, 16), ROWS)],
            x_recv.at[t, x],
        ).start()

    def share(t):
        q = chunks[t]
        for source in range(LOCAL):
            arrived(rows.at[q, core, pl.ds(source * ROWS, ROWS)], x_recv.at[t, source])
        copy = remote(
            rows.at[q, core], rows.at[q, core], twin_send.at[t], twin_recv.at[t], twin
        )
        copy.start()
        pending.append(copy)

    def shared(t):
        arrived(rows.at[chunks[t], 1 - core], twin_recv.at[t])

    lane = pl.multiple_of(core * HALF, HALF)

    def make_strip(k):
        left = rows[k, :, :, pl.ds(lane, HALF)].reshape(2 * OWNED, HALF)
        for f in range(LOCAL):
            right = rows[lax.rem(k + core + f, RING)].reshape(2 * OWNED, CHUNK)
            part[k, :, f * CHUNK : (f + 1) * CHUNK] = lax.dot_general(
                left, right, (((0,), (0,)), ((), ())), preferred_element_type=jnp.float32
            )
        last = lax.rem(k + 4 * (1 - core), RING)
        right = rows[last, :, :, pl.ds(lane, HALF)].reshape(2 * OWNED, HALF)
        part[k, :, WIDE:] = lax.dot_general(
            left, right, (((0,), (0,)), ((), ())), preferred_element_type=jnp.float32
        )

    ways = (1, -1)
    halves = (slice(PART, HALF), slice(0, PART))

    def pieces(way, only):
        return (halves[way],) if only else (halves[way], halves[1 - way])

    def piece_id(piece):
        return 0 if piece.start == 0 else 1

    def send_step(way, t):
        k = turn(z, ways[way] * (4 - t), RING)
        for piece in pieces(way, t == 0):
            h = piece_id(piece)
            value = part[k, piece]
            if t >= 2 or (t == 1 and piece == halves[way]):
                arrived(recv_sum.at[way, t - 1, piece], sum_recv.at[way, t - 1, h])
                value = value + recv_sum[way, t - 1, piece].astype(jnp.float32)
            send_sum[way, t, piece] = value.astype(jnp.bfloat16)
            copy = remote(
                send_sum.at[way, t, piece],
                recv_sum.at[way, t, piece],
                sum_send.at[way, t, h],
                sum_recv.at[way, t, h],
                device(x, y, turn(z, ways[way], RING), core),
            )
            copy.start()
            pending.append(copy)

    for t in range(RING + 2):
        if t < RING:
            pass_on(t)
        if 1 <= t <= RING:
            share(t - 1)
        if t >= 2:
            shared(t - 2)
            if t - 2 == 4:
                make_strip(turn(z, 4, RING))
                send_step(0, 0)
                send_step(1, 0)
            if t - 2 == 5:
                make_strip(turn(z, -3, RING))
            if t - 2 == 6:
                make_strip(turn(z, -2, RING))
                send_step(1, 1)
    make_strip(turn(z, 3, RING))
    send_step(0, 1)

    total = jnp.zeros((1, CHUNK), jnp.float32)
    for q in range(RING):
        values = rows[q].reshape(2 * OWNED, CHUNK).astype(jnp.float32)
        total = total + jnp.sum(values * values, axis=0, keepdims=True)
    squares[z] = jnp.broadcast_to(total[:, :HALF] + total[:, HALF:], (8, HALF))
    for e in range(1, RING):
        copy = remote(
            squares.at[z],
            squares.at[z],
            sq_send.at[e],
            sq_recv.at[e],
            device(x, y, turn(z, e, RING), core),
        )
        copy.start()
        pending.append(copy)

    make_strip(turn(z, 2, RING))
    send_step(1, 2)
    send_step(0, 2)
    make_strip(turn(z, -1, RING))
    make_strip(turn(z, 1, RING))
    send_step(1, 3)
    send_step(0, 3)
    make_strip(z)

    for e in range(1, RING):
        arrived(squares.at[turn(z, -e, RING)], sq_recv.at[e])
    everything = jnp.sum(
        jnp.sum(squares[:, 0, :], axis=0, keepdims=True), axis=1, keepdims=True
    )
    factor = 0.5 * math.sqrt(FF) / jnp.sqrt(everything + 1e-6)
    for q in range(RING):
        normal[:, q * CHUNK : (q + 1) * CHUNK] = (
            rows[q, core].astype(jnp.float32) * factor
        ).astype(jnp.bfloat16)

    def spread_step(way, t):
        k = turn(z, -ways[way] * t, RING)
        for piece in pieces(way, t == 3):
            h = piece_id(piece)
            if t > 0:
                arrived(strips.at[core, k, piece], all_recv.at[way, t - 1, h])
            copy = remote(
                strips.at[core, k, piece],
                strips.at[core, k, piece],
                all_send.at[way, t, h],
                all_recv.at[way, t, h],
                device(x, y, turn(z, ways[way], RING), core),
            )
            copy.start()
            pending.append(copy)
        if t == 3:
            piece = halves[1 - way]
            arrived(strips.at[core, k, piece], all_recv.at[way, t - 1, piece_id(piece)])

    def give_twin(k, n):
        copy = remote(
            strips.at[core, k],
            strips.at[core, k],
            all_twin_send.at[n],
            all_twin_recv.at[n],
            twin,
        )
        copy.start()
        pending.append(copy)

    def lay(which, k):
        at = pl.multiple_of(k * CHUNK + which * HALF, HALF)
        for f in range(LOCAL):
            q = lax.rem(k + which + f, RING)
            block = strips[which, k, :, f * CHUNK : (f + 1) * CHUNK]
            to = pl.multiple_of(q * CHUNK, CHUNK)
            gram[pl.ds(at, HALF), pl.ds(to, CHUNK)] = block
            gram[pl.ds(to, CHUNK), pl.ds(at, HALF)] = block.T
        q = lax.rem(k + 4 * (1 - which), RING)
        to = pl.multiple_of(q * CHUNK + which * HALF, HALF)
        gram[pl.ds(at, HALF), pl.ds(to, HALF)] = strips[which, k, :, WIDE:]

    scale = factor * factor
    for way in range(2):
        for piece in halves:
            arrived(recv_sum.at[way, 3, piece], sum_recv.at[way, 3, piece_id(piece)])
    strips[core, z] = (
        (
            part[z]
            + recv_sum[0, 3].astype(jnp.float32)
            + recv_sum[1, 3].astype(jnp.float32)
        )
        * scale
    ).astype(jnp.bfloat16)

    names = [z]
    for t in range(4):
        spread_step(0, t)
        spread_step(1, t)
        if t == 0:
            give_twin(z, 0)
            lay(core, z)
        else:
            below, above = turn(z, -t, RING), turn(z, t, RING)
            give_twin(below, 2 * t - 1)
            give_twin(above, 2 * t)
            names += [below, above]
            lay(core, below)
            lay(core, above)
            for n in (2 * t - 3, 2 * t - 2) if t > 1 else (0,):
                arrived(strips.at[1 - core, names[n]], all_twin_recv.at[n])
                lay(1 - core, names[n])
    for n in (5, 6):
        arrived(strips.at[1 - core, names[n]], all_twin_recv.at[n])
        lay(1 - core, names[n])
    far = turn(z, 4, RING)
    for way in range(2):
        arrived(strips.at[core, far, halves[way]], all_recv.at[way, 3, piece_id(halves[way])])
    give_twin(far, 7)
    lay(core, far)
    arrived(strips.at[1 - core, far], all_twin_recv.at[7])
    lay(1 - core, far)

    def first(q, carry):
        at = pl.ds(pl.multiple_of(q * CHUNK, CHUNK), CHUNK)
        product[:, at] = jnp.dot(
            normal[...], gram[:, at], preferred_element_type=jnp.float32
        ).astype(jnp.bfloat16)
        return carry

    lax.fori_loop(0, RING, first, 0)

    for q in range(RING):
        at = slice(q * CHUNK, (q + 1) * CHUNK)
        second = jnp.dot(product[...], gram[:, at], preferred_element_type=jnp.float32)
        orthogonal = (
            3.4445 * normal[:, at].astype(jnp.float32)
            - 4.775 * product[:, at].astype(jnp.float32)
            + 2.0315 * second
        )
        done[q] = (orthogonal * math.sqrt(D)).astype(jnp.bfloat16)
        for to in along_x[1:]:
            copy = remote(
                done.at[q, pl.ds(pl.multiple_of(to * ROWS, 16), ROWS)],
                result.at[x, :, at],
                back_send.at[q, to],
                back_recv.at[q, x],
                device(to, y, z, core),
            )
            copy.start()
            pending.append(copy)
        pltpu.make_async_copy(
            done.at[q, pl.ds(pl.multiple_of(x * ROWS, 16), ROWS)],
            result.at[x, :, at],
            back_recv.at[q, x],
        ).start()
    for q in range(RING):
        for source in range(LOCAL):
            arrived(result.at[source, :, q * CHUNK : (q + 1) * CHUNK], back_recv.at[q, source])
    for copy in pending:
        copy.wait_send()


def muon(outgoing):
    dma = pltpu.SemaphoreType.DMA
    bf16, f32 = jnp.bfloat16, jnp.float32
    return pl.pallas_call(
        muon_kernel,
        out_shape=jax.ShapeDtypeStruct((LOCAL, ROWS, FF), bf16),
        in_specs=[pl.BlockSpec(memory_space=pltpu.VMEM)],
        out_specs=pl.BlockSpec(memory_space=pl.ANY),
        scratch_shapes=[
            pltpu.VMEM((RING, LOCAL, ROWS, CHUNK), bf16),
            pltpu.VMEM((RING, 2, OWNED, CHUNK), bf16),
            pltpu.VMEM((RING, 8, 128), f32),
            pltpu.VMEM((RING, HALF, STRIP), f32),
            pltpu.VMEM((2, 4, HALF, STRIP), bf16),
            pltpu.VMEM((2, 4, HALF, STRIP), bf16),
            pltpu.VMEM((2, RING, HALF, STRIP), bf16),
            pltpu.VMEM((FF, FF), bf16),
            pltpu.VMEM((OWNED, FF), bf16),
            pltpu.VMEM((OWNED, FF), bf16),
            pltpu.VMEM((RING, OWNED, CHUNK), bf16),
            dma((RING, LOCAL)),
            dma((RING, LOCAL)),
            dma((RING, LOCAL)),
            dma((RING, LOCAL)),
            dma((RING,)),
            dma((RING,)),
            dma((RING,)),
            dma((RING,)),
            dma((2, 4, 2)),
            dma((2, 4, 2)),
            dma((2, 4, 2)),
            dma((2, 4, 2)),
            dma((RING,)),
            dma((RING,)),
            dma((RING, LOCAL)),
            dma((RING, LOCAL)),
        ],
        compiler_params=pltpu.CompilerParams(
            collective_id=0, has_side_effects=True, vmem_limit_bytes=56 << 20
        ),
        name="muon",
    )(outgoing)


def shards(grad, momentum, placement):
    group = lax.axis_index("expert")
    ids = lax.iota(jnp.int32, LOCAL)
    targets = lax.dynamic_slice_in_dim(placement, group * LOCAL, LOCAL) // LOCAL
    send_slots = jnp.sum((targets[None, :] == ids[:, None]) * ids[None, :], axis=1)
    table = placement.reshape(LOCAL, LOCAL)
    new_slot = jnp.sum(jnp.where(table // LOCAL == group, table % LOCAL, 0), axis=1)
    sources = jnp.sum((new_slot[None, :] == ids[:, None]) * ids[None, :], axis=1)
    momentum_new, outgoing = prepare(send_slots.astype(jnp.int32), grad, momentum)
    update = place(sources.astype(jnp.int32), muon(outgoing))
    return (momentum_new, update)


def solution(mesh):
    return jax.shard_map(
        shards,
        mesh=mesh,
        in_specs=(P("expert", "dp", None), P("expert", "dp", None), P()),
        out_specs=(P("expert", "dp", None), P("expert", "dp", None)),
        check_vma=False,
    )
```

```python
import functools
import math

import jax
import jax.numpy as jnp
from jax import lax
from jax.experimental import pallas as pl
from jax.experimental.pallas import tpu as pltpu
from jax.sharding import PartitionSpec as P

D = 7168
MESH = pl.DeviceIdType.MESH
LOCAL = 4
RING = 8
ROWS = 112
OWNED = LOCAL * ROWS
FF = 2048
CHUNK = FF // RING
HALF = CHUNK // 2
WIDE = LOCAL * CHUNK
STRIP = WIDE + HALF
PIECES = 4
PART = HALF // PIECES


def muon_kernel(
    placement,
    grad,
    momentum,
    update,
    grad_in,
    momentum_in,
    outgoing,
    returned,
    placed,
    by_source,
    rows,
    squares,
    part,
    send_sum,
    recv_sum,
    strips,
    gram,
    normal,
    product,
    done,
    load_sem,
    store_sem,
    y_send,
    y_recv,
    x_send,
    x_recv,
    twin_send,
    twin_recv,
    sq_send,
    sq_recv,
    sum_send,
    sum_recv,
    all_send,
    all_recv,
    all_twin_send,
    all_twin_recv,
    back_send,
    back_recv,
):
    dp = lax.axis_index("dp")
    y = lax.axis_index("expert")
    x, z, core = dp // 16, (dp // 2) % RING, dp % 2

    def device(to_x, to_y, to_z, to_core):
        return (to_x * 16 + to_z * 2 + to_core, to_y)

    def turn(value, by, size):
        return lax.rem(value + (by % size), size)

    def remote(source, target, send, recv, where):
        return pltpu.make_async_remote_copy(
            src_ref=source,
            dst_ref=target,
            send_sem=send,
            recv_sem=recv,
            device_id=where,
            device_id_type=MESH,
        )

    def arrived(ref, sem):
        pltpu.make_async_copy(ref, ref, sem).wait()

    chunks = [turn(z, 4 + t, RING) for t in range(RING)]

    def columns(q):
        return pl.ds(pl.multiple_of(q * CHUNK, CHUNK), CHUNK)

    loads = []
    for t, q in enumerate(chunks):
        pair = [
            pltpu.make_async_copy(grad.at[:, :, columns(q)], grad_in[t], load_sem.at[t, 0]),
            pltpu.make_async_copy(
                momentum.at[:, :, columns(q)], momentum_in[t], load_sem.at[t, 1]
            ),
        ]
        for copy in pair:
            copy.start()
        loads.append(pair)

    chosen, origin = [], []
    for place in range(LOCAL):
        slot, source = jnp.int32(0), jnp.int32(0)
        for j in range(1, LOCAL):
            goes = placement[y * LOCAL + j] // LOCAL
            slot = jnp.where(goes == place, j, slot)
        for e in range(LOCAL, LOCAL * LOCAL):
            source = jnp.where(placement[e] == y * LOCAL + place, e // LOCAL, source)
        chosen.append(slot)
        origin.append(source)

    along_x = [turn(x, e, LOCAL) for e in range(LOCAL)]
    along_y = [turn(y, e, LOCAL) for e in range(LOCAL)]
    twin = device(x, y, z, 1 - core)

    barrier = pltpu.get_barrier_semaphore()
    partners = (
        [device(to, y, z, core) for to in along_x[1:]]
        + [device(x, to, z, core) for to in along_y[1:]]
        + [device(x, y, turn(z, e, RING), core) for e in range(1, RING)]
        + [twin]
    )
    for partner in partners:
        pl.semaphore_signal(barrier, inc=1, device_id=partner, device_id_type=MESH)
    pl.semaphore_wait(barrier, len(partners))

    pending = []

    def depart(t):
        for copy in loads[t]:
            copy.wait()
        q = chunks[t]
        for to in range(LOCAL):
            new = 0.95 * momentum_in[t][chosen[to]] + grad_in[t][chosen[to]].astype(jnp.float32)
            outgoing[q, to] = new.astype(jnp.bfloat16)
        sent = []
        for to in along_y[1:]:
            copy = remote(
                outgoing.at[q, to],
                by_source.at[q, y],
                y_send.at[t, to],
                y_recv.at[t, y],
                device(x, to, z, core),
            )
            copy.start()
            sent.append(copy)
        pltpu.make_async_copy(outgoing.at[q, y], by_source.at[q, y], y_recv.at[t, y]).start()
        return sent

    def pass_on(t):
        q = chunks[t]
        for to in along_x[1:]:
            arrived(by_source.at[q, to], y_recv.at[t, to])
            copy = remote(
                by_source.at[q, to],
                rows.at[q, core, pl.ds(pl.multiple_of(x * ROWS, 16), ROWS)],
                x_send.at[t, to],
                x_recv.at[t, x],
                device(to, y, z, core),
            )
            copy.start()
            pending.append(copy)
        arrived(by_source.at[q, x], y_recv.at[t, x])
        pltpu.make_async_copy(
            by_source.at[q, x],
            rows.at[q, core, pl.ds(pl.multiple_of(x * ROWS, 16), ROWS)],
            x_recv.at[t, x],
        ).start()

    def share(t):
        q = chunks[t]
        for source in range(LOCAL):
            arrived(rows.at[q, core, pl.ds(source * ROWS, ROWS)], x_recv.at[t, source])
        copy = remote(
            rows.at[q, core], rows.at[q, core], twin_send.at[t], twin_recv.at[t], twin
        )
        copy.start()
        pending.append(copy)

    def shared(t):
        arrived(rows.at[chunks[t], 1 - core], twin_recv.at[t])

    lane = pl.multiple_of(core * HALF, HALF)

    def make_strip(k):
        left = rows[k, :, :, pl.ds(lane, HALF)].reshape(2 * OWNED, HALF)
        for f in range(LOCAL):
            right = rows[lax.rem(k + core + f, RING)].reshape(2 * OWNED, CHUNK)
            part[k, :, f * CHUNK : (f + 1) * CHUNK] = lax.dot_general(
                left, right, (((0,), (0,)), ((), ())), preferred_element_type=jnp.float32
            )
        last = lax.rem(k + 4 * (1 - core), RING)
        right = rows[last, :, :, pl.ds(lane, HALF)].reshape(2 * OWNED, HALF)
        part[k, :, WIDE:] = lax.dot_general(
            left, right, (((0,), (0,)), ((), ())), preferred_element_type=jnp.float32
        )

    ways = (1, -1)
    rows_of = [slice(n * PART, (n + 1) * PART) for n in range(PIECES)]
    half = PIECES // 2
    order = (tuple(range(half, PIECES)) + tuple(range(half)), tuple(range(PIECES)))

    def from_far(way):
        return order[way][:half]

    def send_piece(way, t, n):
        k = turn(z, ways[way] * (4 - t), RING)
        piece = rows_of[n]
        value = part[k, piece]
        if t >= 2 or (t == 1 and n in from_far(way)):
            arrived(recv_sum.at[way, t - 1, piece], sum_recv.at[way, t - 1, n])
            value = value + recv_sum[way, t - 1, piece].astype(jnp.float32)
        send_sum[way, t, piece] = value.astype(jnp.bfloat16)
        copy = remote(
            send_sum.at[way, t, piece],
            recv_sum.at[way, t, piece],
            sum_send.at[way, t, n],
            sum_recv.at[way, t, n],
            device(x, y, turn(z, ways[way], RING), core),
        )
        copy.start()
        pending.append(copy)

    def send_step(t, which=(0, 1)):
        for i in range(PIECES if t else half):
            for way in which:
                send_piece(way, t, order[way][i])

    in_flight = [depart(0), depart(1)]
    for t in range(RING + 2):
        if t < RING:
            pass_on(t)
            for copy in in_flight[t]:
                copy.wait_send()
            if t + 2 < RING:
                in_flight.append(depart(t + 2))
        if 1 <= t <= RING:
            share(t - 1)
        if t >= 2:
            shared(t - 2)
            if t - 2 == 4:
                make_strip(turn(z, 4, RING))
                send_step(0)
            if t - 2 == 5:
                make_strip(turn(z, -3, RING))
            if t - 2 == 6:
                make_strip(turn(z, -2, RING))
                send_step(1, (1,))
    make_strip(turn(z, 3, RING))
    send_step(1, (0,))

    total = jnp.zeros((1, CHUNK), jnp.float32)
    for q in range(RING):
        values = rows[q].reshape(2 * OWNED, CHUNK).astype(jnp.float32)
        total = total + jnp.sum(values * values, axis=0, keepdims=True)
    squares[z] = jnp.broadcast_to(total[:, :HALF] + total[:, HALF:], (8, HALF))
    for e in range(1, RING):
        copy = remote(
            squares.at[z],
            squares.at[z],
            sq_send.at[e],
            sq_recv.at[e],
            device(x, y, turn(z, e, RING), core),
        )
        copy.start()
        pending.append(copy)

    make_strip(turn(z, 2, RING))
    send_step(2)
    make_strip(turn(z, -1, RING))
    make_strip(turn(z, 1, RING))
    send_step(3)
    make_strip(z)

    for e in range(1, RING):
        arrived(squares.at[turn(z, -e, RING)], sq_recv.at[e])
    everything = jnp.sum(
        jnp.sum(squares[:, 0, :], axis=0, keepdims=True), axis=1, keepdims=True
    )
    factor = 0.5 * math.sqrt(FF) / jnp.sqrt(everything + 1e-6)
    for q in range(RING):
        normal[:, q * CHUNK : (q + 1) * CHUNK] = (
            rows[q, core].astype(jnp.float32) * factor
        ).astype(jnp.bfloat16)

    def spread_piece(way, t, n):
        k = turn(z, -ways[way] * t, RING)
        piece = rows_of[n]
        if t > 0:
            arrived(strips.at[core, k, piece], all_recv.at[way, t - 1, n])
        if t == 3 and n not in from_far(way):
            return None
        copy = remote(
            strips.at[core, k, piece],
            strips.at[core, k, piece],
            all_send.at[way, t, n],
            all_recv.at[way, t, n],
            device(x, y, turn(z, ways[way], RING), core),
        )
        copy.start()
        return copy

    def give_twin(k, n):
        copy = remote(
            strips.at[core, k],
            strips.at[core, k],
            all_twin_send.at[n],
            all_twin_recv.at[n],
            twin,
        )
        copy.start()
        pending.append(copy)

    def lay(which, k):
        at = pl.multiple_of(k * CHUNK + which * HALF, HALF)
        for f in range(LOCAL):
            q = lax.rem(k + which + f, RING)
            block = strips[which, k, :, f * CHUNK : (f + 1) * CHUNK]
            to = pl.multiple_of(q * CHUNK, CHUNK)
            gram[pl.ds(at, HALF), pl.ds(to, CHUNK)] = block
            gram[pl.ds(to, CHUNK), pl.ds(at, HALF)] = block.T
        q = lax.rem(k + 4 * (1 - which), RING)
        to = pl.multiple_of(q * CHUNK + which * HALF, HALF)
        gram[pl.ds(at, HALF), pl.ds(to, HALF)] = strips[which, k, :, WIDE:]

    scale = factor * factor
    sent = []
    for n in range(PIECES):
        piece = rows_of[n]
        for way in range(2):
            arrived(recv_sum.at[way, 3, piece], sum_recv.at[way, 3, n])
        strips[core, z, piece] = (
            (
                part[z, piece]
                + recv_sum[0, 3, piece].astype(jnp.float32)
                + recv_sum[1, 3, piece].astype(jnp.float32)
            )
            * scale
        ).astype(jnp.bfloat16)
        for way in range(2):
            sent.append(spread_piece(way, 0, n))
    give_twin(z, 0)
    lay(core, z)
    pending.extend(sent)

    def lay_twin(k, n):
        arrived(strips.at[1 - core, k], all_twin_recv.at[n])
        lay(1 - core, k)

    tasks = [lambda: lay_twin(z, 0)]
    for t in range(1, 4):
        for i in range(PIECES):
            for way in range(2):
                copy = spread_piece(way, t, order[way][i])
                if copy is not None:
                    pending.append(copy)
            if tasks:
                tasks.pop(0)()
        below, above = turn(z, -t, RING), turn(z, t, RING)
        give_twin(below, 2 * t - 1)
        give_twin(above, 2 * t)
        tasks += [
            functools.partial(lay, core, below),
            functools.partial(lay, core, above),
            functools.partial(lay_twin, below, 2 * t - 1),
            functools.partial(lay_twin, above, 2 * t),
        ]
    for task in tasks:
        task()
    far = turn(z, 4, RING)
    for way in range(2):
        for n in from_far(way):
            arrived(strips.at[core, far, rows_of[n]], all_recv.at[way, 3, n])
    give_twin(far, 7)
    lay(core, far)
    lay_twin(far, 7)

    def first(q, carry):
        at = pl.ds(pl.multiple_of(q * CHUNK, CHUNK), CHUNK)
        product[:, at] = jnp.dot(
            normal[...], gram[:, at], preferred_element_type=jnp.float32
        ).astype(jnp.bfloat16)
        return carry

    lax.fori_loop(0, RING, first, 0)

    for q in range(RING):
        at = slice(q * CHUNK, (q + 1) * CHUNK)
        second = jnp.dot(product[...], gram[:, at], preferred_element_type=jnp.float32)
        orthogonal = (
            3.4445 * normal[:, at].astype(jnp.float32)
            - 4.775 * product[:, at].astype(jnp.float32)
            + 2.0315 * second
        )
        done[q] = (orthogonal * math.sqrt(D)).astype(jnp.bfloat16)
        for to in along_x[1:]:
            copy = remote(
                done.at[q, pl.ds(pl.multiple_of(to * ROWS, 16), ROWS)],
                returned[q].at[x],
                back_send.at[q, to],
                back_recv.at[q, x],
                device(to, y, z, core),
            )
            copy.start()
            pending.append(copy)
        pltpu.make_async_copy(
            done.at[q, pl.ds(pl.multiple_of(x * ROWS, 16), ROWS)],
            returned[q].at[x],
            back_recv.at[q, x],
        ).start()
    stores = []
    for q in range(RING):
        at = slice(q * CHUNK, (q + 1) * CHUNK)
        for source in range(LOCAL):
            arrived(returned[q].at[source], back_recv.at[q, source])
        for place in range(LOCAL):
            placed[place, :, at] = returned[q][origin[place]]
        copy = pltpu.make_async_copy(placed.at[:, :, at], update.at[:, :, at], store_sem.at[q])
        copy.start()
        stores.append(copy)
    for copy in stores:
        copy.wait()
    for copy in pending:
        copy.wait_send()


def muon(placement, grad, momentum):
    dma = pltpu.SemaphoreType.DMA
    bf16, f32 = jnp.bfloat16, jnp.float32
    return pl.pallas_call(
        muon_kernel,
        out_shape=jax.ShapeDtypeStruct((LOCAL, ROWS, FF), bf16),
        in_specs=[
            pl.BlockSpec(memory_space=pltpu.SMEM),
            pl.BlockSpec(memory_space=pl.ANY),
            pl.BlockSpec(memory_space=pl.ANY),
        ],
        out_specs=pl.BlockSpec(memory_space=pl.ANY),
        scratch_shapes=[
            [pltpu.VMEM((LOCAL, ROWS, CHUNK), bf16)] * RING,
            [pltpu.VMEM((LOCAL, ROWS, CHUNK), f32)] * RING,
            pltpu.VMEM((RING, LOCAL, ROWS, CHUNK), bf16),
            [pltpu.VMEM((LOCAL, ROWS, CHUNK), bf16)] * RING,
            pltpu.VMEM((LOCAL, ROWS, FF), bf16),
            pltpu.VMEM((RING, LOCAL, ROWS, CHUNK), bf16),
            pltpu.VMEM((RING, 2, OWNED, CHUNK), bf16),
            pltpu.VMEM((RING, 8, 128), f32),
            pltpu.VMEM((RING, HALF, STRIP), f32),
            pltpu.VMEM((2, 4, HALF, STRIP), bf16),
            pltpu.VMEM((2, 4, HALF, STRIP), bf16),
            pltpu.VMEM((2, RING, HALF, STRIP), bf16),
            pltpu.VMEM((FF, FF), bf16),
            pltpu.VMEM((OWNED, FF), bf16),
            pltpu.VMEM((OWNED, FF), bf16),
            pltpu.VMEM((RING, OWNED, CHUNK), bf16),
            dma((RING, 2)),
            dma((RING,)),
            dma((RING, LOCAL)),
            dma((RING, LOCAL)),
            dma((RING, LOCAL)),
            dma((RING, LOCAL)),
            dma((RING,)),
            dma((RING,)),
            dma((RING,)),
            dma((RING,)),
            dma((2, 4, PIECES)),
            dma((2, 4, PIECES)),
            dma((2, 4, PIECES)),
            dma((2, 4, PIECES)),
            dma((RING,)),
            dma((RING,)),
            dma((RING, LOCAL)),
            dma((RING, LOCAL)),
        ],
        compiler_params=pltpu.CompilerParams(
            collective_id=0, has_side_effects=True, vmem_limit_bytes=60 << 20
        ),
        name="muon",
    )(placement, grad, momentum)


def shards(grad, momentum, placement):
    update = muon(placement, grad, momentum)
    momentum_new = 0.95 * momentum + grad.astype(jnp.float32)
    return (momentum_new, update)


def solution(mesh):
    return jax.shard_map(
        shards,
        mesh=mesh,
        in_specs=(P("expert", "dp", None), P("expert", "dp", None), P()),
        out_specs=(P("expert", "dp", None), P("expert", "dp", None)),
        check_vma=False,
    )
```

```python
import functools
import math

import jax
import jax.numpy as jnp
from jax import lax
from jax.experimental import pallas as pl
from jax.experimental.pallas import tpu as pltpu
from jax.sharding import PartitionSpec as P

D = 7168
MESH = pl.DeviceIdType.MESH
LOCAL = 4
RING = 8
ROWS = 112
OWNED = LOCAL * ROWS
FF = 2048
CHUNK = FF // RING
HALF = CHUNK // 2
WIDE = LOCAL * CHUNK
STRIP = WIDE + HALF
PIECES = 5
COLUMNS = tuple(slice(f * CHUNK, min((f + 1) * CHUNK, STRIP)) for f in range(PIECES))
ORDER = (4, 5, 6, 3, 7, 2, 0, 1)
FAR = ((0, 1), (2, 3, 4))


def owner(way, step):
    return (step - 4 if way else 4 - step) % RING


def plan():
    took, delay = (0.5, 0.5, 0.5, 0.5, 0.25), 0.9
    events = []
    for way in range(2):
        todo = [(t, f) for t in range(4) for f in range(PIECES) if t or f in FAR[way]]
        came, free = {}, 0.0
        while todo:
            options = []
            for t, f in todo:
                k = owner(way, t)
                ready = 1.0 + max(ORDER.index(k), ORDER.index((k + f) % RING))
                if t > 1 or (t == 1 and f in FAR[way]):
                    ready = max(ready, came.get((t - 1, f), 1e9))
                options.append((max(ready, free), t, f, ready))
            start, t, f, ready = min(options)
            todo.remove((t, f))
            free = start + took[f]
            came[t, f] = free + delay
            events.append((ready, way, t, f))
    return sorted(events)


def muon_kernel(
    placement,
    grad,
    momentum,
    update,
    momentum_new,
    grad_in,
    momentum_in,
    outgoing,
    returned,
    placed,
    by_source,
    rows,
    squares,
    turned,
    part,
    send_sum,
    recv_sum,
    strips,
    gram,
    normal,
    early,
    product,
    done,
    load_sem,
    store_sem,
    new_sem,
    y_send,
    y_recv,
    x_send,
    x_recv,
    twin_send,
    twin_recv,
    sq_send,
    sq_recv,
    sum_send,
    sum_recv,
    all_send,
    all_recv,
    all_twin_send,
    all_twin_recv,
    back_send,
    back_recv,
):
    dp = lax.axis_index("dp")
    y = lax.axis_index("expert")
    x, z, core = dp // 16, (dp // 2) % RING, dp % 2

    def device(to_x, to_y, to_z, to_core):
        return (to_x * 16 + to_z * 2 + to_core, to_y)

    def turn(value, by, size):
        return lax.rem(value + (by % size), size)

    def remote(source, target, send, recv, where):
        return pltpu.make_async_remote_copy(
            src_ref=source,
            dst_ref=target,
            send_sem=send,
            recv_sem=recv,
            device_id=where,
            device_id_type=MESH,
        )

    def arrived(ref, sem):
        pltpu.make_async_copy(ref, ref, sem).wait()

    chunks = [turn(z, j, RING) for j in ORDER]

    def columns(q):
        return pl.ds(pl.multiple_of(q * CHUNK, CHUNK), CHUNK)

    loads = []
    for t, q in enumerate(chunks):
        pair = [
            pltpu.make_async_copy(grad.at[:, :, columns(q)], grad_in[t], load_sem.at[t, 0]),
            pltpu.make_async_copy(
                momentum.at[:, :, columns(q)], momentum_in[t], load_sem.at[t, 1]
            ),
        ]
        for copy in pair:
            copy.start()
        loads.append(pair)

    chosen, origin = [], []
    for place in range(LOCAL):
        slot, source = jnp.int32(0), jnp.int32(0)
        for j in range(1, LOCAL):
            goes = placement[y * LOCAL + j] // LOCAL
            slot = jnp.where(goes == place, j, slot)
        for e in range(LOCAL, LOCAL * LOCAL):
            source = jnp.where(placement[e] == y * LOCAL + place, e // LOCAL, source)
        chosen.append(slot)
        origin.append(source)

    along_x = [turn(x, e, LOCAL) for e in range(LOCAL)]
    along_y = [turn(y, e, LOCAL) for e in range(LOCAL)]
    twin = device(x, y, z, 1 - core)

    barrier = pltpu.get_barrier_semaphore()
    partners = (
        [device(to, y, z, core) for to in along_x[1:]]
        + [device(x, to, z, core) for to in along_y[1:]]
        + [device(x, y, turn(z, e, RING), core) for e in range(1, RING)]
        + [twin]
    )
    for partner in partners:
        pl.semaphore_signal(barrier, inc=1, device_id=partner, device_id_type=MESH)
    pl.semaphore_wait(barrier, len(partners))

    pending = []

    def depart(t):
        for copy in loads[t]:
            copy.wait()
        q = chunks[t]
        momentum_in[t][...] = 0.95 * momentum_in[t][...] + grad_in[t][...].astype(jnp.float32)
        for to in range(LOCAL):
            outgoing[q, to] = momentum_in[t][chosen[to]].astype(jnp.bfloat16)
        copy = pltpu.make_async_copy(
            momentum_in[t], momentum_new.at[:, :, columns(q)], new_sem.at[t]
        )
        copy.start()
        stores.append(copy)
        sent = []
        for to in along_y[1:]:
            copy = remote(
                outgoing.at[q, to],
                by_source.at[q, y],
                y_send.at[t, to],
                y_recv.at[t, y],
                device(x, to, z, core),
            )
            copy.start()
            sent.append(copy)
        pltpu.make_async_copy(outgoing.at[q, y], by_source.at[q, y], y_recv.at[t, y]).start()
        return sent

    def pass_on(t):
        q = chunks[t]
        for to in along_x[1:]:
            arrived(by_source.at[q, to], y_recv.at[t, to])
            copy = remote(
                by_source.at[q, to],
                rows.at[q, core, pl.ds(pl.multiple_of(x * ROWS, 16), ROWS)],
                x_send.at[t, to],
                x_recv.at[t, x],
                device(to, y, z, core),
            )
            copy.start()
            pending.append(copy)
        arrived(by_source.at[q, x], y_recv.at[t, x])
        pltpu.make_async_copy(
            by_source.at[q, x],
            rows.at[q, core, pl.ds(pl.multiple_of(x * ROWS, 16), ROWS)],
            x_recv.at[t, x],
        ).start()

    def share(t):
        q = chunks[t]
        for source in range(LOCAL):
            arrived(rows.at[q, core, pl.ds(source * ROWS, ROWS)], x_recv.at[t, source])
        copy = remote(
            rows.at[q, core], rows.at[q, core], twin_send.at[t], twin_recv.at[t], twin
        )
        copy.start()
        pending.append(copy)

    def shared(t):
        arrived(rows.at[chunks[t], 1 - core], twin_recv.at[t])

    lane = pl.multiple_of(core * HALF, HALF)

    def last_lane(which, k):
        return pl.multiple_of(lax.rem(which + k // LOCAL, 2) * HALF, HALF)

    def make_piece(j, f):
        k, q = turn(z, j, RING), turn(z, j + f, RING)
        if f < LOCAL:
            right = rows[q]
        else:
            right = rows[q, :, :, pl.ds(last_lane(core, k), HALF)]
        part[j, :, COLUMNS[f]] = jnp.dot(
            turned[j], right.reshape(2 * OWNED, -1), preferred_element_type=jnp.float32
        )

    ways = (1, -1)

    def send_piece(way, t, f):
        j, at = owner(way, t), COLUMNS[f]
        value = part[j, :, at]
        if t > 1 or (t == 1 and f in FAR[way]):
            arrived(recv_sum.at[way, t - 1, :, at], sum_recv.at[way, t - 1, f])
            value = value + recv_sum[way, t - 1, :, at].astype(jnp.float32)
        send_sum[way, t, :, at] = value.astype(jnp.bfloat16)
        copy = remote(
            send_sum.at[way, t, :, at],
            recv_sum.at[way, t, :, at],
            sum_send.at[way, t, f],
            sum_recv.at[way, t, f],
            device(x, y, turn(z, ways[way], RING), core),
        )
        copy.start()
        pending.append(copy)

    sends = plan()
    total = jnp.zeros((1, CHUNK), jnp.float32)
    stores = []
    in_flight = [depart(0), depart(1)]
    for t in range(RING + 2):
        if t < RING:
            pass_on(t)
            for copy in in_flight[t]:
                copy.wait_send()
            if t + 2 < RING:
                in_flight.append(depart(t + 2))
        if 1 <= t <= RING:
            share(t - 1)
        if t >= 2:
            shared(t - 2)
            q, j = chunks[t - 2], ORDER[t - 2]
            turned[j] = rows[q, :, :, pl.ds(lane, HALF)].reshape(2 * OWNED, HALF).T
            for i in ORDER[: t - 1]:
                for f in range(PIECES):
                    if (i == j or (i + f) % RING == j) and (i + f) % RING in ORDER[: t - 1]:
                        make_piece(i, f)
            while sends and sends[0][0] < t - 0.5:
                send_piece(*sends.pop(0)[1:])
            values = rows[q].reshape(2 * OWNED, CHUNK).astype(jnp.float32)
            total = total + jnp.sum(values * values, axis=0, keepdims=True)

    squares[z] = jnp.broadcast_to(total[:, :HALF] + total[:, HALF:], (8, HALF))
    for e in range(1, RING):
        copy = remote(
            squares.at[z],
            squares.at[z],
            sq_send.at[e],
            sq_recv.at[e],
            device(x, y, turn(z, e, RING), core),
        )
        copy.start()
        pending.append(copy)

    for event in sends:
        send_piece(*event[1:])

    for e in range(1, RING):
        arrived(squares.at[turn(z, -e, RING)], sq_recv.at[e])
    everything = jnp.sum(
        jnp.sum(squares[:, 0, :], axis=0, keepdims=True), axis=1, keepdims=True
    )
    factor = 0.5 * math.sqrt(FF) / jnp.sqrt(everything + 1e-6)
    def spread_piece(way, t, f):
        k, at = turn(z, -ways[way] * t, RING), COLUMNS[f]
        if t > 0:
            arrived(strips.at[core, k, :, at], all_recv.at[way, t - 1, f])
        if t == 3 and f not in FAR[way]:
            return None
        copy = remote(
            strips.at[core, k, :, at],
            strips.at[core, k, :, at],
            all_send.at[way, t, f],
            all_recv.at[way, t, f],
            device(x, y, turn(z, ways[way], RING), core),
        )
        copy.start()
        return copy

    def give_twin(k, n):
        copy = remote(
            strips.at[core, k],
            strips.at[core, k],
            all_twin_send.at[n],
            all_twin_recv.at[n],
            twin,
        )
        copy.start()
        pending.append(copy)

    def spot(j):
        return (j + 3) % RING * CHUNK

    def lay(which, j):
        k = turn(z, j, RING)
        at = pl.multiple_of(spot(j) + which * HALF, HALF)
        for f in range(PIECES):
            to, size = spot(j + f), CHUNK
            if f == LOCAL:
                to, size = pl.multiple_of(to + last_lane(which, k), HALF), HALF
            block = strips[which, k, :, COLUMNS[f]]
            gram[pl.ds(at, HALF), pl.ds(to, size)] = block
            if f > 0:
                gram[pl.ds(to, size), pl.ds(at, HALF)] = block.T

    scale = factor * factor
    sent = []
    for f in range(PIECES):
        at = COLUMNS[f]
        for way in range(2):
            arrived(recv_sum.at[way, 3, :, at], sum_recv.at[way, 3, f])
        strips[core, z, :, at] = (
            (
                part[0, :, at]
                + recv_sum[0, 3, :, at].astype(jnp.float32)
                + recv_sum[1, 3, :, at].astype(jnp.float32)
            )
            * scale
        ).astype(jnp.bfloat16)
        for way in range(2):
            sent.append(spread_piece(way, 0, f))
    give_twin(z, 0)
    lay(core, 0)
    pending.extend(sent)

    def lay_twin(j, n):
        arrived(strips.at[1 - core, turn(z, j, RING)], all_twin_recv.at[n])
        lay(1 - core, j)

    def scale_rows(j):
        values = rows[turn(z, j, RING), core].astype(jnp.float32)
        normal[:, spot(j) : spot(j) + CHUNK] = (values * factor).astype(jnp.bfloat16)

    tasks = [functools.partial(scale_rows, j) for j in range(RING)]
    tasks.append(lambda: lay_twin(0, 0))
    for t in range(1, 4):
        for i in range(PIECES):
            for way in range(2):
                copy = spread_piece(way, t, i)
                if copy is not None:
                    pending.append(copy)
            for task in tasks[: 2 if t == 1 else 1]:
                task()
            tasks = tasks[2 if t == 1 else 1 :]
        give_twin(turn(z, -t, RING), 2 * t - 1)
        give_twin(turn(z, t, RING), 2 * t)
        tasks += [
            functools.partial(lay, core, -t),
            functools.partial(lay, core, t),
            functools.partial(lay_twin, -t, 2 * t - 1),
            functools.partial(lay_twin, t, 2 * t),
        ]
    for task in tasks:
        task()

    near = FF - CHUNK

    def begin(p):
        early[p] = jnp.dot(
            normal[:, :near],
            gram[:near, p * CHUNK : (p + 1) * CHUNK],
            preferred_element_type=jnp.float32,
        )

    for p in range(4):
        begin(p)
    far = turn(z, 4, RING)
    for way in range(2):
        for f in FAR[way]:
            arrived(strips.at[core, far, :, COLUMNS[f]], all_recv.at[way, 3, f])
    give_twin(far, 7)
    lay(core, 4)
    for p in range(4, RING - 1):
        begin(p)
    lay_twin(4, 7)
    for p in range(RING):
        at = slice(p * CHUNK, (p + 1) * CHUNK)
        if p < RING - 1:
            value = early[p] + jnp.dot(
                normal[:, near:], gram[near:, at], preferred_element_type=jnp.float32
            )
        else:
            value = jnp.dot(normal[...], gram[:, at], preferred_element_type=jnp.float32)
        product[:, at] = value.astype(jnp.bfloat16)

    for q in range(RING):
        at = slice(q * CHUNK, (q + 1) * CHUNK)
        second = jnp.dot(product[...], gram[:, at], preferred_element_type=jnp.float32)
        orthogonal = (
            3.4445 * normal[:, at].astype(jnp.float32)
            - 4.775 * product[:, at].astype(jnp.float32)
            + 2.0315 * second
        )
        done[q] = (orthogonal * math.sqrt(D)).astype(jnp.bfloat16)
        for to in along_x[1:]:
            copy = remote(
                done.at[q, pl.ds(pl.multiple_of(to * ROWS, 16), ROWS)],
                returned[q].at[x],
                back_send.at[q, to],
                back_recv.at[q, x],
                device(to, y, z, core),
            )
            copy.start()
            pending.append(copy)
        pltpu.make_async_copy(
            done.at[q, pl.ds(pl.multiple_of(x * ROWS, 16), ROWS)],
            returned[q].at[x],
            back_recv.at[q, x],
        ).start()
    for p in range(RING):
        at = columns(turn(z, p + 5, RING))
        for source in range(LOCAL):
            arrived(returned[p].at[source], back_recv.at[p, source])
        for place in range(LOCAL):
            placed[place, :, at] = returned[p][origin[place]]
        copy = pltpu.make_async_copy(placed.at[:, :, at], update.at[:, :, at], store_sem.at[p])
        copy.start()
        stores.append(copy)
    for copy in stores:
        copy.wait()
    for copy in pending:
        copy.wait_send()


def muon(placement, grad, momentum):
    dma = pltpu.SemaphoreType.DMA
    bf16, f32 = jnp.bfloat16, jnp.float32
    return pl.pallas_call(
        muon_kernel,
        out_shape=[
            jax.ShapeDtypeStruct((LOCAL, ROWS, FF), bf16),
            jax.ShapeDtypeStruct((LOCAL, ROWS, FF), f32),
        ],
        in_specs=[
            pl.BlockSpec(memory_space=pltpu.SMEM),
            pl.BlockSpec(memory_space=pl.ANY),
            pl.BlockSpec(memory_space=pl.ANY),
        ],
        out_specs=[pl.BlockSpec(memory_space=pl.ANY)] * 2,
        scratch_shapes=[
            [pltpu.VMEM((LOCAL, ROWS, CHUNK), bf16)] * RING,
            [pltpu.VMEM((LOCAL, ROWS, CHUNK), f32)] * RING,
            pltpu.VMEM((RING, LOCAL, ROWS, CHUNK), bf16),
            [pltpu.VMEM((LOCAL, ROWS, CHUNK), bf16)] * RING,
            pltpu.VMEM((LOCAL, ROWS, FF), bf16),
            pltpu.VMEM((RING, LOCAL, ROWS, CHUNK), bf16),
            pltpu.VMEM((RING, 2, OWNED, CHUNK), bf16),
            pltpu.VMEM((RING, 8, 128), f32),
            pltpu.VMEM((RING, HALF, 2 * OWNED), bf16),
            pltpu.VMEM((RING, HALF, STRIP), f32),
            pltpu.VMEM((2, 4, HALF, STRIP), bf16),
            pltpu.VMEM((2, 4, HALF, STRIP), bf16),
            pltpu.VMEM((2, RING, HALF, STRIP), bf16),
            pltpu.VMEM((FF, FF), bf16),
            pltpu.VMEM((OWNED, FF), bf16),
            pltpu.VMEM((RING - 1, OWNED, CHUNK), f32),
            pltpu.VMEM((OWNED, FF), bf16),
            pltpu.VMEM((RING, OWNED, CHUNK), bf16),
            dma((RING, 2)),
            dma((RING,)),
            dma((RING,)),
            dma((RING, LOCAL)),
            dma((RING, LOCAL)),
            dma((RING, LOCAL)),
            dma((RING, LOCAL)),
            dma((RING,)),
            dma((RING,)),
            dma((RING,)),
            dma((RING,)),
            dma((2, 4, PIECES)),
            dma((2, 4, PIECES)),
            dma((2, 4, PIECES)),
            dma((2, 4, PIECES)),
            dma((RING,)),
            dma((RING,)),
            dma((RING, LOCAL)),
            dma((RING, LOCAL)),
        ],
        compiler_params=pltpu.CompilerParams(
            collective_id=0, has_side_effects=True, vmem_limit_bytes=60 << 20
        ),
        name="muon",
    )(placement, grad, momentum)


def settle_kernel(update_from, momentum_from, update, momentum_new, held_update, held, sems):
    copies = []
    for j in range(LOCAL):
        first = [
            pltpu.make_async_copy(momentum_from.at[j], held.at[j], sems.at[0, j]),
            pltpu.make_async_copy(update_from.at[j], held_update.at[j], sems.at[1, j]),
        ]
        then = [
            pltpu.make_async_copy(held.at[j], momentum_new.at[j], sems.at[2, j]),
            pltpu.make_async_copy(held_update.at[j], update.at[j], sems.at[3, j]),
        ]
        for copy in first:
            copy.start()
        copies.append((first, then))
    for first, then in copies:
        for i in range(2):
            first[i].wait()
            then[i].start()
    for _, then in copies:
        for copy in then:
            copy.wait()


def settle(update, momentum_new):
    anywhere = pl.BlockSpec(memory_space=pl.ANY)
    return pl.pallas_call(
        settle_kernel,
        out_shape=[
            jax.ShapeDtypeStruct((LOCAL, ROWS, FF), jnp.bfloat16),
            jax.ShapeDtypeStruct((LOCAL, ROWS, FF), jnp.float32),
        ],
        in_specs=[anywhere] * 2,
        out_specs=[anywhere] * 2,
        scratch_shapes=[
            pltpu.VMEM((LOCAL, ROWS, FF), jnp.bfloat16),
            pltpu.VMEM((LOCAL, ROWS, FF), jnp.float32),
            pltpu.SemaphoreType.DMA((4, LOCAL)),
        ],
        compiler_params=pltpu.CompilerParams(vmem_limit_bytes=60 << 20),
        name="settle",
    )(update, momentum_new)


def shards(grad, momentum, placement):
    update, momentum_new = settle(*muon(placement, grad, momentum))
    return (momentum_new, update)


def solution(mesh):
    return jax.shard_map(
        shards,
        mesh=mesh,
        in_specs=(P("expert", "dp", None), P("expert", "dp", None), P()),
        out_specs=(P("expert", "dp", None), P("expert", "dp", None)),
        check_vma=False,
    )
```

```python
import functools
import math

import jax
import jax.numpy as jnp
from jax import lax
from jax.experimental import pallas as pl
from jax.experimental.pallas import tpu as pltpu
from jax.sharding import PartitionSpec as P

D = 7168
MESH = pl.DeviceIdType.MESH
LOCAL = 4
RING = 8
ROWS = 112
OWNED = LOCAL * ROWS
FF = 2048
CHUNK = FF // RING
HALF = CHUNK // 2
WIDE = LOCAL * CHUNK
STRIP = WIDE + HALF
PIECES = 5
COLUMNS = tuple(slice(f * CHUNK, min((f + 1) * CHUNK, STRIP)) for f in range(PIECES))
ORDER = (4, 5, 6, 3, 7, 2, 0, 1)
FAR = ((0, 1), (2, 3, 4))


def owner(way, step):
    return (step - 4 if way else 4 - step) % RING


def plan():
    took, delay = (0.38, 0.38, 0.38, 0.38, 0.19), 0.7
    events = []
    for way in range(2):
        todo = [(t, f) for t in range(4) for f in range(PIECES) if t or f in FAR[way]]
        came, free = {}, 0.0
        while todo:
            options = []
            for t, f in todo:
                k = owner(way, t)
                ready = 1.0 + max(ORDER.index(k), ORDER.index((k + f) % RING))
                if t > 1 or (t == 1 and f in FAR[way]):
                    ready = max(ready, came.get((t - 1, f), 1e9))
                options.append((max(ready, free), t, f, ready))
            start, t, f, ready = min(options)
            todo.remove((t, f))
            free = start + took[f]
            came[t, f] = free + delay
            events.append((ready, way, t, f))
    return sorted(events)


def muon_kernel(
    placement,
    grad,
    momentum,
    update,
    momentum_new,
    grad_in,
    momentum_in,
    outgoing,
    returned,
    placed,
    by_source,
    rows,
    squares,
    turned,
    part,
    send_sum,
    recv_sum,
    strips,
    gram,
    normal,
    early,
    product,
    done,
    load_sem,
    store_sem,
    new_sem,
    y_send,
    y_recv,
    x_send,
    x_recv,
    twin_send,
    twin_recv,
    sq_send,
    sq_recv,
    sum_send,
    sum_recv,
    all_send,
    all_recv,
    all_twin_send,
    all_twin_recv,
    back_send,
    back_recv,
):
    dp = lax.axis_index("dp")
    y = lax.axis_index("expert")
    x, z, core = dp // 16, (dp // 2) % RING, dp % 2

    def device(to_x, to_y, to_z, to_core):
        return (to_x * 16 + to_z * 2 + to_core, to_y)

    def turn(value, by, size):
        return lax.rem(value + (by % size), size)

    def remote(source, target, send, recv, where):
        return pltpu.make_async_remote_copy(
            src_ref=source,
            dst_ref=target,
            send_sem=send,
            recv_sem=recv,
            device_id=where,
            device_id_type=MESH,
        )

    def arrived(ref, sem):
        pltpu.make_async_copy(ref, ref, sem).wait()

    chunks = [turn(z, j, RING) for j in ORDER]

    def columns(q):
        return pl.ds(pl.multiple_of(q * CHUNK, CHUNK), CHUNK)

    loads = []
    for t, q in enumerate(chunks):
        pair = [
            pltpu.make_async_copy(grad.at[:, :, columns(q)], grad_in[t], load_sem.at[t, 0]),
            pltpu.make_async_copy(
                momentum.at[:, :, columns(q)], momentum_in[t], load_sem.at[t, 1]
            ),
        ]
        for copy in pair:
            copy.start()
        loads.append(pair)

    chosen, origin = [], []
    for place in range(LOCAL):
        slot, source = jnp.int32(0), jnp.int32(0)
        for j in range(1, LOCAL):
            goes = placement[y * LOCAL + j] // LOCAL
            slot = jnp.where(goes == place, j, slot)
        for e in range(LOCAL, LOCAL * LOCAL):
            source = jnp.where(placement[e] == y * LOCAL + place, e // LOCAL, source)
        chosen.append(slot)
        origin.append(source)

    along_x = [turn(x, e, LOCAL) for e in (0, 2, 1, 3)]
    along_y = [turn(y, e, LOCAL) for e in (0, 2, 1, 3)]
    twin = device(x, y, z, 1 - core)

    barrier = pltpu.get_barrier_semaphore()
    partners = (
        [device(to, y, z, core) for to in along_x[1:]]
        + [device(x, to, z, core) for to in along_y[1:]]
        + [device(x, y, turn(z, e, RING), core) for e in range(1, RING)]
        + [twin]
    )
    for partner in partners:
        pl.semaphore_signal(barrier, inc=1, device_id=partner, device_id_type=MESH)
    pl.semaphore_wait(barrier, len(partners))

    pending = []

    def depart(t):
        for copy in loads[t]:
            copy.wait()
        q = chunks[t]
        momentum_in[t][...] = 0.95 * momentum_in[t][...] + grad_in[t][...].astype(jnp.float32)
        for to in range(LOCAL):
            outgoing[q, to] = momentum_in[t][chosen[to]].astype(jnp.bfloat16)
        copy = pltpu.make_async_copy(
            momentum_in[t], momentum_new.at[:, :, columns(q)], new_sem.at[t]
        )
        copy.start()
        stores.append(copy)
        sent = []
        for to in along_y[1:]:
            copy = remote(
                outgoing.at[q, to],
                by_source.at[q, y],
                y_send.at[t, to],
                y_recv.at[t, y],
                device(x, to, z, core),
            )
            copy.start()
            sent.append(copy)
        pltpu.make_async_copy(outgoing.at[q, y], by_source.at[q, y], y_recv.at[t, y]).start()
        return sent

    def pass_on(t):
        q = chunks[t]
        for to in along_x[1:]:
            arrived(by_source.at[q, to], y_recv.at[t, to])
            copy = remote(
                by_source.at[q, to],
                rows.at[q, core, pl.ds(pl.multiple_of(x * ROWS, 16), ROWS)],
                x_send.at[t, to],
                x_recv.at[t, x],
                device(to, y, z, core),
            )
            copy.start()
            pending.append(copy)
        arrived(by_source.at[q, x], y_recv.at[t, x])
        pltpu.make_async_copy(
            by_source.at[q, x],
            rows.at[q, core, pl.ds(pl.multiple_of(x * ROWS, 16), ROWS)],
            x_recv.at[t, x],
        ).start()

    def share(t):
        q = chunks[t]
        for source in range(LOCAL):
            arrived(rows.at[q, core, pl.ds(source * ROWS, ROWS)], x_recv.at[t, source])
        copy = remote(
            rows.at[q, core], rows.at[q, core], twin_send.at[t], twin_recv.at[t], twin
        )
        copy.start()
        pending.append(copy)

    def shared(t):
        arrived(rows.at[chunks[t], 1 - core], twin_recv.at[t])

    lane = pl.multiple_of(core * HALF, HALF)

    def last_lane(which, k):
        return pl.multiple_of(lax.rem(which + k // LOCAL, 2) * HALF, HALF)

    def make_piece(j, f):
        k, q = turn(z, j, RING), turn(z, j + f, RING)
        if f < LOCAL:
            right = rows[q]
        else:
            right = rows[q, :, :, pl.ds(last_lane(core, k), HALF)]
        part[j, :, COLUMNS[f]] = jnp.dot(
            turned[j], right.reshape(2 * OWNED, -1), preferred_element_type=jnp.float32
        )

    ways = (1, -1)

    def send_piece(way, t, f):
        j, at = owner(way, t), COLUMNS[f]
        value = part[j, :, at]
        if t > 1 or (t == 1 and f in FAR[way]):
            arrived(recv_sum.at[way, t - 1, :, at], sum_recv.at[way, t - 1, f])
            value = value + recv_sum[way, t - 1, :, at].astype(jnp.float32)
        send_sum[way, t, :, at] = value.astype(jnp.bfloat16)
        copy = remote(
            send_sum.at[way, t, :, at],
            recv_sum.at[way, t, :, at],
            sum_send.at[way, t, f],
            sum_recv.at[way, t, f],
            device(x, y, turn(z, ways[way], RING), core),
        )
        copy.start()
        pending.append(copy)

    sends = plan()
    total = jnp.zeros((1, CHUNK), jnp.float32)
    stores = []
    in_flight = [depart(0), depart(1)]
    for t in range(RING + 2):
        if t < RING:
            pass_on(t)
            for copy in in_flight[t]:
                copy.wait_send()
            if t + 2 < RING:
                in_flight.append(depart(t + 2))
        if 1 <= t <= RING:
            share(t - 1)
        if t >= 2:
            shared(t - 2)
            q, j = chunks[t - 2], ORDER[t - 2]
            turned[j] = rows[q, :, :, pl.ds(lane, HALF)].reshape(2 * OWNED, HALF).T
            for i in ORDER[: t - 1]:
                for f in range(PIECES):
                    if (i == j or (i + f) % RING == j) and (i + f) % RING in ORDER[: t - 1]:
                        make_piece(i, f)
            while sends and sends[0][0] < t - 0.9:
                send_piece(*sends.pop(0)[1:])
            values = rows[q].reshape(2 * OWNED, CHUNK).astype(jnp.float32)
            total = total + jnp.sum(values * values, axis=0, keepdims=True)

    squares[z] = jnp.broadcast_to(total[:, :HALF] + total[:, HALF:], (8, HALF))
    for e in range(1, RING):
        copy = remote(
            squares.at[z],
            squares.at[z],
            sq_send.at[e],
            sq_recv.at[e],
            device(x, y, turn(z, e, RING), core),
        )
        copy.start()
        pending.append(copy)

    for event in sends:
        send_piece(*event[1:])

    for e in range(1, RING):
        arrived(squares.at[turn(z, -e, RING)], sq_recv.at[e])
    everything = jnp.sum(
        jnp.sum(squares[:, 0, :], axis=0, keepdims=True), axis=1, keepdims=True
    )
    factor = 0.5 * math.sqrt(FF) / jnp.sqrt(everything + 1e-6)
    def spread_piece(way, t, f):
        k, at = turn(z, -ways[way] * t, RING), COLUMNS[f]
        if t > 0:
            arrived(strips.at[core, k, :, at], all_recv.at[way, t - 1, f])
        if t == 3 and f not in FAR[way]:
            return None
        copy = remote(
            strips.at[core, k, :, at],
            strips.at[core, k, :, at],
            all_send.at[way, t, f],
            all_recv.at[way, t, f],
            device(x, y, turn(z, ways[way], RING), core),
        )
        copy.start()
        return copy

    def give_twin(k, n):
        copy = remote(
            strips.at[core, k],
            strips.at[core, k],
            all_twin_send.at[n],
            all_twin_recv.at[n],
            twin,
        )
        copy.start()
        pending.append(copy)

    def spot(j):
        return (j + 3) % RING * CHUNK

    def lay(which, j):
        k = turn(z, j, RING)
        at = pl.multiple_of(spot(j) + which * HALF, HALF)
        for f in range(PIECES):
            to, size = spot(j + f), CHUNK
            if f == LOCAL:
                to, size = pl.multiple_of(to + last_lane(which, k), HALF), HALF
            block = strips[which, k, :, COLUMNS[f]]
            gram[pl.ds(at, HALF), pl.ds(to, size)] = block
            if f > 0:
                gram[pl.ds(to, size), pl.ds(at, HALF)] = block.T

    scale = factor * factor
    sent = []
    for f in range(PIECES):
        at = COLUMNS[f]
        for way in range(2):
            arrived(recv_sum.at[way, 3, :, at], sum_recv.at[way, 3, f])
        strips[core, z, :, at] = (
            (
                part[0, :, at]
                + recv_sum[0, 3, :, at].astype(jnp.float32)
                + recv_sum[1, 3, :, at].astype(jnp.float32)
            )
            * scale
        ).astype(jnp.bfloat16)
        for way in range(2):
            sent.append(spread_piece(way, 0, f))
    give_twin(z, 0)
    lay(core, 0)
    pending.extend(sent)

    def lay_twin(j, n):
        arrived(strips.at[1 - core, turn(z, j, RING)], all_twin_recv.at[n])
        lay(1 - core, j)

    def scale_rows(j):
        values = rows[turn(z, j, RING), core].astype(jnp.float32)
        normal[:, spot(j) : spot(j) + CHUNK] = (values * factor).astype(jnp.bfloat16)

    tasks = [functools.partial(scale_rows, j) for j in range(RING)]
    tasks.append(lambda: lay_twin(0, 0))
    for t in range(1, 4):
        for i in range(PIECES):
            for way in range(2):
                copy = spread_piece(way, t, i)
                if copy is not None:
                    pending.append(copy)
            for task in tasks[: 2 if t == 1 else 1]:
                task()
            tasks = tasks[2 if t == 1 else 1 :]
        give_twin(turn(z, -t, RING), 2 * t - 1)
        give_twin(turn(z, t, RING), 2 * t)
        tasks += [
            functools.partial(lay, core, -t),
            functools.partial(lay, core, t),
            functools.partial(lay_twin, -t, 2 * t - 1),
            functools.partial(lay_twin, t, 2 * t),
        ]
    for task in tasks:
        task()

    near = FF - CHUNK

    def begin(p):
        early[p] = jnp.dot(
            normal[:, :near],
            gram[:near, p * CHUNK : (p + 1) * CHUNK],
            preferred_element_type=jnp.float32,
        )

    for p in range(4):
        begin(p)
    far = turn(z, 4, RING)
    for way in range(2):
        for f in FAR[way]:
            arrived(strips.at[core, far, :, COLUMNS[f]], all_recv.at[way, 3, f])
    give_twin(far, 7)
    lay(core, 4)
    for p in range(4, RING - 1):
        begin(p)
    lay_twin(4, 7)
    for p in range(RING):
        at = slice(p * CHUNK, (p + 1) * CHUNK)
        if p < RING - 1:
            value = early[p] + jnp.dot(
                normal[:, near:], gram[near:, at], preferred_element_type=jnp.float32
            )
        else:
            value = jnp.dot(normal[...], gram[:, at], preferred_element_type=jnp.float32)
        product[:, at] = value.astype(jnp.bfloat16)

    early_sends = len(pending)
    for q in range(RING):
        at = slice(q * CHUNK, (q + 1) * CHUNK)
        second = jnp.dot(product[...], gram[:, at], preferred_element_type=jnp.float32)
        orthogonal = (
            3.4445 * normal[:, at].astype(jnp.float32)
            - 4.775 * product[:, at].astype(jnp.float32)
            + 2.0315 * second
        )
        done[q] = (orthogonal * math.sqrt(D)).astype(jnp.bfloat16)
        for to in along_x[1:]:
            copy = remote(
                done.at[q, pl.ds(pl.multiple_of(to * ROWS, 16), ROWS)],
                returned[q].at[x],
                back_send.at[q, to],
                back_recv.at[q, x],
                device(to, y, z, core),
            )
            copy.start()
            pending.append(copy)
        pltpu.make_async_copy(
            done.at[q, pl.ds(pl.multiple_of(x * ROWS, 16), ROWS)],
            returned[q].at[x],
            back_recv.at[q, x],
        ).start()
    for copy in pending[:early_sends]:
        copy.wait_send()
    for p in range(RING):
        at = columns(turn(z, p + 5, RING))
        for source in range(LOCAL):
            arrived(returned[p].at[source], back_recv.at[p, source])
        for place in range(LOCAL):
            placed[place, :, at] = returned[p][origin[place]]
        copy = pltpu.make_async_copy(placed.at[:, :, at], update.at[:, :, at], store_sem.at[p])
        copy.start()
        stores.append(copy)
    for copy in stores:
        copy.wait()
    for copy in pending[early_sends:]:
        copy.wait_send()


def muon(placement, grad, momentum):
    dma = pltpu.SemaphoreType.DMA
    bf16, f32 = jnp.bfloat16, jnp.float32
    return pl.pallas_call(
        muon_kernel,
        out_shape=[
            jax.ShapeDtypeStruct((LOCAL, ROWS, FF), bf16),
            jax.ShapeDtypeStruct((LOCAL, ROWS, FF), f32),
        ],
        in_specs=[
            pl.BlockSpec(memory_space=pltpu.SMEM),
            pl.BlockSpec(memory_space=pl.ANY),
            pl.BlockSpec(memory_space=pl.ANY),
        ],
        out_specs=[pl.BlockSpec(memory_space=pl.ANY)] * 2,
        scratch_shapes=[
            [pltpu.VMEM((LOCAL, ROWS, CHUNK), bf16)] * RING,
            [pltpu.VMEM((LOCAL, ROWS, CHUNK), f32)] * RING,
            pltpu.VMEM((RING, LOCAL, ROWS, CHUNK), bf16),
            [pltpu.VMEM((LOCAL, ROWS, CHUNK), bf16)] * RING,
            pltpu.VMEM((LOCAL, ROWS, FF), bf16),
            pltpu.VMEM((RING, LOCAL, ROWS, CHUNK), bf16),
            pltpu.VMEM((RING, 2, OWNED, CHUNK), bf16),
            pltpu.VMEM((RING, 8, 128), f32),
            pltpu.VMEM((RING, HALF, 2 * OWNED), bf16),
            pltpu.VMEM((RING, HALF, STRIP), f32),
            pltpu.VMEM((2, 4, HALF, STRIP), bf16),
            pltpu.VMEM((2, 4, HALF, STRIP), bf16),
            pltpu.VMEM((2, RING, HALF, STRIP), bf16),
            pltpu.VMEM((FF, FF), bf16),
            pltpu.VMEM((OWNED, FF), bf16),
            pltpu.VMEM((RING - 1, OWNED, CHUNK), f32),
            pltpu.VMEM((OWNED, FF), bf16),
            pltpu.VMEM((RING, OWNED, CHUNK), bf16),
            dma((RING, 2)),
            dma((RING,)),
            dma((RING,)),
            dma((RING, LOCAL)),
            dma((RING, LOCAL)),
            dma((RING, LOCAL)),
            dma((RING, LOCAL)),
            dma((RING,)),
            dma((RING,)),
            dma((RING,)),
            dma((RING,)),
            dma((2, 4, PIECES)),
            dma((2, 4, PIECES)),
            dma((2, 4, PIECES)),
            dma((2, 4, PIECES)),
            dma((RING,)),
            dma((RING,)),
            dma((RING, LOCAL)),
            dma((RING, LOCAL)),
        ],
        compiler_params=pltpu.CompilerParams(
            collective_id=0, has_side_effects=True, vmem_limit_bytes=60 << 20
        ),
        name="muon",
    )(placement, grad, momentum)


def settle_kernel(update_from, momentum_from, update, momentum_new, held_update, held, sems):
    copies = []
    for j in range(LOCAL):
        first = [
            pltpu.make_async_copy(momentum_from.at[j], held.at[j], sems.at[0, j]),
            pltpu.make_async_copy(update_from.at[j], held_update.at[j], sems.at[1, j]),
        ]
        then = [
            pltpu.make_async_copy(held.at[j], momentum_new.at[j], sems.at[2, j]),
            pltpu.make_async_copy(held_update.at[j], update.at[j], sems.at[3, j]),
        ]
        for copy in first:
            copy.start()
        copies.append((first, then))
    for first, then in copies:
        for i in range(2):
            first[i].wait()
            then[i].start()
    for _, then in copies:
        for copy in then:
            copy.wait()


def settle(update, momentum_new):
    anywhere = pl.BlockSpec(memory_space=pl.ANY)
    return pl.pallas_call(
        settle_kernel,
        out_shape=[
            jax.ShapeDtypeStruct((LOCAL, ROWS, FF), jnp.bfloat16),
            jax.ShapeDtypeStruct((LOCAL, ROWS, FF), jnp.float32),
        ],
        in_specs=[anywhere] * 2,
        out_specs=[anywhere] * 2,
        scratch_shapes=[
            pltpu.VMEM((LOCAL, ROWS, FF), jnp.bfloat16),
            pltpu.VMEM((LOCAL, ROWS, FF), jnp.float32),
            pltpu.SemaphoreType.DMA((4, LOCAL)),
        ],
        compiler_params=pltpu.CompilerParams(vmem_limit_bytes=60 << 20),
        name="settle",
    )(update, momentum_new)


def shards(grad, momentum, placement):
    update, momentum_new = settle(*muon(placement, grad, momentum))
    return (momentum_new, update)


def solution(mesh):
    return jax.shard_map(
        shards,
        mesh=mesh,
        in_specs=(P("expert", "dp", None), P("expert", "dp", None), P()),
        out_specs=(P("expert", "dp", None), P("expert", "dp", None)),
        check_vma=False,
    )
```
